32 devices in a mesh: tm: 4 (over y, x), space: 8 (over z, core).
Axes of the slice: x: 2, y: 2, z: 4, core: 2. Of those that a mesh axis runs over, the one named last changes fastest.
Arguments:
- queries: bfloat16 [8, 1024, 1536], P('tm', 'space'), may hold values from -110 to 110
- keys: bfloat16 [8, 1024, 1536], P('tm', 'space'), may hold values from -5.1 to 5.1
- values: bfloat16 [8, 1024, 1536], P('tm', 'space'), may hold values from -15 to 15
- tile_mask: int32 [8, 8, 5, 5], P('tm', 'space'), may hold values from 0 to 1, as said below
Outputs:
- attended: bfloat16 [8, 1024, 1536], P('tm', 'space')
The draws below stay inside these ranges and needn't reach their ends.
Inputs may be any that keep to these rules, and one draw needn't show every extreme that they name: tile_mask[i, b, 2 + d, 2 + e] is 1 where tile (i, b) attends tile (i + d, b + e). It is 0 where |e| > 2 >> |d| or where the key tile lies outside the 8 x 8 tiles, and 1 for d = e = 0.
All inputs are finite; a program needn't handle non-finite values.
Results may differ from the reference program's by a relative error of at most 0.012.
Values may be sent and summed in bfloat16 or wider, within the bound.
A program may use at most 192 MiB of HBM per device.

```python
import math
import jax
import jax.numpy as jnp
from jax import lax

H = 12
HD = 128
BLK = 128
TR = 2
W = 2
FRAMES = 8
NB = 8
ROWS = 1024


def key_field(key):
    shape = (FRAMES, ROWS, H * HD)
    base = jax.random.truncated_normal(jax.random.fold_in(key, 11), -5.0, 5.0, shape, jnp.float32)
    return base


def draw_keys(key, part):
    return key_field(key).astype(jnp.bfloat16)


def draw_queries(key, part):
    shape = (FRAMES, ROWS, H * HD)
    drawn = 2.0 * jax.random.truncated_normal(jax.random.fold_in(key, 13), -5.0, 5.0, shape, jnp.float32)
    return drawn.astype(jnp.bfloat16)


def draw_tile_mask(key, part):
    shape = (FRAMES, NB, 2 * TR + 1, 2 * W + 1)
    level_bits = jax.random.randint(jax.random.fold_in(key, 21), (FRAMES, 1, 1, 1), 0, 4)
    level = jnp.left_shift(jnp.ones_like(level_bits), level_bits)
    frame_index = jax.lax.broadcasted_iota(jnp.int32, shape, 0)
    block_index = jax.lax.broadcasted_iota(jnp.int32, shape, 1)
    d = jax.lax.broadcasted_iota(jnp.int32, shape, 2) - TR
    e = jax.lax.broadcasted_iota(jnp.int32, shape, 3) - W
    level = jnp.where(frame_index == FRAMES // 2, 8, level)
    draw_roll = jax.random.randint(jax.random.fold_in(key, 22), shape, 0, 8)
    kept = draw_roll < level
    inside_band = jnp.abs(e) <= jnp.right_shift(jnp.full(shape, W, jnp.int32), jnp.abs(d))
    valid = (frame_index + d >= 0) & (frame_index + d < FRAMES) & (block_index + e >= 0) & (block_index + e < NB)
    center = (d == 0) & (e == 0)
    return jnp.where(center | kept & inside_band & valid, 1, 0).astype(jnp.int32)


def shard_levels(key, dims, split, smallest, high):
    gain, own = 1.0, jax.random.fold_in(key, 6)
    for axis_at, shards_of in split:
        heights = jnp.exp(jax.random.uniform(jax.random.fold_in(own, axis_at), (shards_of,), jnp.float32, smallest / len(split), high / len(split)))
        gain = gain * jnp.repeat(heights, dims[axis_at] // shards_of).reshape([-1 if axis == axis_at else 1 for axis in range(len(dims))])
    return gain


def scatter_about(key, extent, scale, limit, shards=(), kind=jnp.bfloat16):
    values = scale * jax.random.normal(key, extent, jnp.float32)
    if shards:
        values = values * shard_levels(key, extent, shards, -0.22, 0.18)
    return jnp.clip(values, -limit, limit).astype(kind)


def setup_inputs(seed: int = 0) -> dict:
    key_list = jax.random.split(jax.random.key(seed), 5)
    return {
        "queries": draw_queries(jax.random.fold_in(key_list[4], 71), 0),
        "keys": draw_keys(jax.random.fold_in(key_list[4], 71), 0),
        "values": scatter_about(key_list[2], (FRAMES, ROWS, H * HD), 3.0, 15.0, ((0, 4), (1, 8))),
        "tile_mask": draw_tile_mask(jax.random.fold_in(key_list[4], 71), 0),
    }


def band_list():
    pairs = []
    for d in range(-TR, TR + 1):
        spread = W >> abs(d)
        for e in range(-spread, spread + 1):
            pairs.append((d, e))
    return pairs

def reference(queries, keys, values, tile_mask):
    score_scale = 1.0 / math.sqrt(HD)
    pairs = band_list()

    def one_frame(index):
        query = lax.dynamic_index_in_dim(queries, index, 0, keepdims=False)
        query = query.reshape(NB, BLK, H, HD).astype(jnp.float32)
        frame_flags = lax.dynamic_index_in_dim(tile_mask, index, 0, keepdims=False)
        score_list = []
        value_list = []
        for d, e in pairs:
            source = jnp.clip(index + d, 0, FRAMES - 1).astype(jnp.int32)
            key_frame = lax.dynamic_index_in_dim(keys, source, 0, keepdims=False).reshape(NB, BLK, H, HD)
            key_frame = jnp.roll(key_frame, -e, axis=0).astype(jnp.float32)
            value_frame = lax.dynamic_index_in_dim(values, source, 0, keepdims=False).reshape(NB, BLK, H, HD)
            value_frame = jnp.roll(value_frame, -e, axis=0).astype(jnp.float32)
            scores = jnp.einsum('bqhc,bkhc->bhqk', query, key_frame) * score_scale
            kept = frame_flags[:, TR + d, W + e] > 0
            scores = jnp.where(kept[:, None, None, None], scores, -jnp.inf)
            score_list.append(scores)
            value_list.append(value_frame)
        scores = jnp.concatenate(score_list, axis=3)
        row_max = lax.optimization_barrier(jnp.max(scores, axis=3, keepdims=True))
        weights = jnp.exp(scores - row_max)
        denominator = lax.optimization_barrier(jnp.sum(weights, axis=3))
        rounded = weights.astype(jnp.bfloat16).astype(jnp.float32)
        summed = jnp.zeros((NB, BLK, H, HD), jnp.float32)
        for number in range(len(pairs)):
            portion = rounded[..., number * BLK:(number + 1) * BLK]
            summed = summed + jnp.einsum('bhqk,bkhc->bqhc', portion, value_list[number])
        result = summed / jnp.transpose(denominator, (0, 2, 1))[..., None]
        return result.reshape(ROWS, H * HD).astype(jnp.bfloat16)
    return lax.map(one_frame, jnp.arange(FRAMES, dtype=jnp.int32))
```

```python
import functools
import math

import jax
import jax.numpy as jnp
from jax import lax
from jax.experimental import pallas as pl
from jax.experimental.pallas import tpu as pltpu
from jax.sharding import PartitionSpec as P

HD = 128
BLK = 128
TR = 2
W = 2
MESH = pl.DeviceIdType.MESH
SEGMENTS = ((0, -2, 5), (-1, -1, 3), (1, -1, 3), (-2, 0, 1), (2, 0, 1))
ROWS = 16


def kernel(groups, chips, nh, q_ref, k_ref, v_ref, b_ref, o_ref,
           kv, qb, bb, ob, send_sem, near, zsem, ysem, fsem, qsem, bsem, osem):
    tm, sp = lax.axis_index("tm"), lax.axis_index("space")
    k, p = tm // 2, tm % 2
    z, c = sp // 2, sp % 2
    has_z = {-1: z > 0, 1: z < chips - 1}
    has_k = {-1: k > 0, 1: k < groups - 1}

    def device(t, s):
        return {"tm": t, "space": s}

    def cols(pp, cc, j):
        return pl.ds(pl.multiple_of(((2 * pp + cc) * nh + j) * HD, HD), HD)

    def quad():
        for dp, dc in ((0, 0), (0, 1), (1, 0), (1, 1)):
            yield dp + dc == 0, (p + dp) % 2, (c + dc) % 2

    barrier = pltpu.get_barrier_semaphore()

    def greet(dev):
        pl.semaphore_signal(barrier, inc=1, device_id=dev, device_id_type=MESH)

    for own, pp, cc in quad():
        if not own:
            greet(device(2 * k + pp, 2 * z + cc))
    for s in (-1, 1):
        @pl.when(has_z[s])
        def _():
            for cc in range(2):
                greet(device(tm, 2 * (z + s) + cc))

        @pl.when(has_k[s])
        def _():
            greet(device(tm + 2 * s, sp))
    count = 3
    for s in (-1, 1):
        count = count + 2 * has_z[s].astype(jnp.int32) + has_k[s].astype(jnp.int32)
    pl.semaphore_wait(barrier, count)

    sent = []

    def send(cond, src, dst, sem, dev):
        copy = pltpu.make_async_remote_copy(
            src_ref=src, dst_ref=dst, send_sem=send_sem.at[len(sent)], recv_sem=sem,
            device_id=dev, device_id_type=MESH)
        if cond is None:
            copy.start()
        else:
            pl.when(cond)(copy.start)
        sent.append((cond, copy))

    def to_quad(own, src, dst, sem, pp, cc):
        if own:
            pltpu.make_async_copy(src, dst, sem).start()
        else:
            send(None, src, dst, sem, device(2 * k + pp, 2 * z + cc))

    def arrived(ref, sem):
        pltpu.make_async_copy(ref, ref, sem).wait()

    mine = pl.ds(2 + 2 * p, 2)
    other = pl.ds(4 - 2 * p, 2)
    inputs = (k_ref, v_ref)

    for j in range(nh):
        for own, pp, cc in quad():
            for i in range(2):
                to_quad(own, inputs[i].at[:, :, cols(pp, cc, j)], kv.at[j, i, mine, 2 + c],
                        near.at[j], pp, cc)
        for s in (-1, 1):
            tile = c if s == 1 else 4 + c
            for cc in range(2):
                for i in range(2):
                    send(has_z[s], inputs[i].at[:, :, cols(p, cc, j)], kv.at[j, i, mine, tile],
                         zsem.at[j, (1 - s) // 2], device(tm, 2 * (z + s) + cc))
    for own, pp, cc in quad():
        to_quad(own, b_ref, bb.at[pl.ds(2 * p, 2), c], bsem, pp, cc)
    for j in range(nh):
        for own, pp, cc in quad():
            to_quad(own, q_ref.at[:, :, cols(pp, cc, j)], qb.at[j, pl.ds(2 * p, 2), c],
                    qsem.at[j], pp, cc)

    for s in (-1, 1):
        tiles = slice(0, 2) if s == -1 else slice(4, 6)
        tile = 1 if s == -1 else 4
        frames = slice(0, 2) if s == -1 else slice(6, 8)
        frame = 1 if s == -1 else 6

        @pl.when(jnp.logical_not(has_z[s]))
        def _():
            for j in range(nh):
                for i in range(2):
                    kv[j, i, 2:6, tiles] = jnp.zeros((4, 2, BLK, HD), kv.dtype)
                    for f in (1, 6):
                        kv[j, i, f, tile] = jnp.zeros((BLK, HD), kv.dtype)

        @pl.when(jnp.logical_not(has_k[s]))
        def _():
            for j in range(nh):
                for i in range(2):
                    kv[j, i, frames, 2:4] = jnp.zeros((2, 2, BLK, HD), kv.dtype)

        for u in (-1, 1):
            @pl.when(jnp.logical_and(jnp.logical_not(has_k[s]), has_z[u]))
            def _():
                for j in range(nh):
                    for i in range(2):
                        kv[j, i, frame, 1 if u == -1 else 4] = jnp.zeros((BLK, HD), kv.dtype)

    for j in range(nh):
        arrived(kv.at[j, :, 2:6, 2:4], near.at[j])
        for s in (-1, 1):
            tiles = pl.ds(0 if s == 1 else 4, 2)
            send(has_z[s], kv.at[j, :, other, pl.ds(2, 2)], kv.at[j, :, other, tiles],
                 zsem.at[j, (1 - s) // 2], device(tm, 2 * (z + s) + c))
        for s in (-1, 1):
            source, target = (4, 0) if s == 1 else (2, 6)
            send(has_k[s], kv.at[j, :, pl.ds(source, 2), pl.ds(2, 2)],
                 kv.at[j, :, pl.ds(target, 2), pl.ds(2, 2)],
                 ysem.at[j, (1 - s) // 2], device(tm + 2 * s, sp))

    factor = math.log2(math.e) / math.sqrt(HD)

    def attend(j, f, b):
        query = qb[j, f, b]
        parts, row = [], 0
        best = None
        for d, e, n in SEGMENTS:
            keys = kv[j, 0, f + 2 + d, b + 2 + e:b + 2 + e + n].reshape(n * BLK, HD)
            scores = lax.dot_general(query, keys, (((1,), (1,)), ((), ())),
                                     preferred_element_type=jnp.float32)
            for t in range(n):
                part = scores[:, t * BLK:(t + 1) * BLK] + bb[f, b, row:row + 1, :]
                parts.append(part)
                best = part if best is None else jnp.maximum(best, part)
                row += 1
        row_max = jnp.max(best, axis=1, keepdims=True)
        total, summed, at = None, None, 0
        for d, e, n in SEGMENTS:
            rounded = []
            for t in range(n):
                weights = jnp.exp2((parts[at] - row_max) * factor)
                total = weights if total is None else total + weights
                rounded.append(weights.astype(jnp.bfloat16))
                at += 1
            rounded = rounded[0] if n == 1 else jnp.concatenate(rounded, axis=1)
            vals = kv[j, 1, f + 2 + d, b + 2 + e:b + 2 + e + n].reshape(n * BLK, HD)
            product = jnp.dot(rounded, vals, preferred_element_type=jnp.float32)
            summed = product if summed is None else summed + product
        denominator = jnp.sum(total, axis=1, keepdims=True)
        ob[j, f, b] = (summed / denominator).astype(jnp.bfloat16)

    for j in range(nh):
        for s in (-1, 1):
            tile = 1 if s == -1 else 4
            side = (1 + s) // 2
            tiles = pl.ds(0 if s == -1 else 4, 2)

            @pl.when(has_z[s])
            def _():
                arrived(kv.at[j, :, 2:6, tiles], zsem.at[j, side])
            for u in (-1, 1):
                source, target = (5, 1) if u == 1 else (2, 6)
                send(jnp.logical_and(has_z[s], has_k[u]), kv.at[j, :, source, tile],
                     kv.at[j, :, target, tile], fsem.at[j, (1 - u) // 2, side],
                     device(tm + 2 * u, sp))
        if j == 0:
            arrived(bb, bsem)
        arrived(qb.at[j], qsem.at[j])
        for u in (-1, 1):
            @pl.when(has_k[u])
            def _():
                arrived(kv.at[j, :, pl.ds(0 if u == -1 else 6, 2), pl.ds(2, 2)],
                        ysem.at[j, (1 + u) // 2])
            for s in (-1, 1):
                @pl.when(jnp.logical_and(has_k[u], has_z[s]))
                def _():
                    arrived(kv.at[j, :, 1 if u == -1 else 6, 1 if s == -1 else 4],
                            fsem.at[j, (1 + u) // 2, (1 + s) // 2])

        def frame_step(f, carry):
            for b in range(2):
                attend(j, f, b)
            return carry

        lax.fori_loop(0, 4, frame_step, 0)
        for own, pp, cc in quad():
            to_quad(own, ob.at[j, pl.ds(2 * pp, 2), cc], o_ref.at[:, :, cols(p, c, j)],
                    osem, pp, cc)

    arrived(o_ref, osem)
    for cond, copy in sent:
        if cond is None:
            copy.wait_send()
        else:
            pl.when(cond)(copy.wait_send)


def on_device(groups, chips, queries, keys, values, tile_mask):
    nh = queries.shape[2] // HD // 4
    flags = [tile_mask[:, 0, TR + d, W + e + t] for d, e, n in SEGMENTS for t in range(n)]
    flags = jnp.stack(flags + [flags[0]] * (ROWS - len(flags)), axis=1)
    bias = jnp.where(flags > 0, 0.0, -jnp.inf).astype(jnp.float32)
    bias = jnp.broadcast_to(bias[:, :, None], bias.shape + (BLK,))
    hbm = pl.BlockSpec(memory_space=pl.ANY)
    vmem = pl.BlockSpec(memory_space=pltpu.VMEM)
    dma = pltpu.SemaphoreType.DMA
    return pl.pallas_call(
        functools.partial(kernel, groups, chips, nh),
        out_shape=jax.ShapeDtypeStruct(queries.shape, queries.dtype),
        in_specs=[hbm, hbm, hbm, vmem],
        out_specs=hbm,
        scratch_shapes=[
            pltpu.VMEM((nh, 2, 8, 6, BLK, HD), jnp.bfloat16),
            pltpu.VMEM((nh, 4, 2, BLK, HD), jnp.bfloat16),
            pltpu.VMEM((4, 2, ROWS, BLK), jnp.float32),
            pltpu.VMEM((nh, 4, 2, BLK, HD), jnp.bfloat16),
            dma((32 * nh + 4,)),
            dma((nh,)),
            dma((nh, 2)),
            dma((nh, 2)),
            dma((nh, 2, 2)),
            dma((nh,)),
            dma,
            dma,
        ],
        compiler_params=pltpu.CompilerParams(
            collective_id=0, has_side_effects=True, vmem_limit_bytes=48 * 2**20
        ),
    )(queries, keys, values, bias)


def solution(mesh):
    in_specs = (
        P("tm", "space", None),
        P("tm", "space", None),
        P("tm", "space", None),
        P("tm", "space", None, None),
    )
    out_specs = P("tm", "space", None)
    return jax.shard_map(
        functools.partial(on_device, mesh.shape["tm"] // 2, mesh.shape["space"] // 2),
        mesh=mesh, in_specs=in_specs, out_specs=out_specs, check_vma=False
    )
```

```python
import functools
import math

import jax
import jax.numpy as jnp
from jax import lax
from jax.experimental import pallas as pl
from jax.experimental.pallas import tpu as pltpu
from jax.sharding import PartitionSpec as P

HD = 128
BLK = 128
TR = 2
W = 2
MESH = pl.DeviceIdType.MESH
SEGMENTS = ((0, -2, 5), (-1, -1, 3), (1, -1, 3), (-2, 0, 1), (2, 0, 1))
ROWS = 16


def kernel(groups, chips, nh, q_ref, k_ref, v_ref, m_ref, o_ref,
           kv, qb, bb, bias, ob, send_sem, near, zsem, dsem, ysem, fsem, qsem, bsem, osem):
    tm, sp = lax.axis_index("tm"), lax.axis_index("space")
    k, p = tm // 2, tm % 2
    z, c = sp // 2, sp % 2
    has_z = {-1: z > 0, 1: z < chips - 1}
    has_k = {-1: k > 0, 1: k < groups - 1}

    def device(t, s):
        return {"tm": t, "space": s}

    def cols(pp, cc, j):
        return pl.ds(pl.multiple_of(((2 * pp + cc) * nh + j) * HD, HD), HD)

    def quad():
        for dp, dc in ((0, 0), (0, 1), (1, 0), (1, 1)):
            yield dp + dc == 0, (p + dp) % 2, (c + dc) % 2

    barrier = pltpu.get_barrier_semaphore()

    def greet(dev):
        pl.semaphore_signal(barrier, inc=1, device_id=dev, device_id_type=MESH)

    for own, pp, cc in quad():
        if not own:
            greet(device(2 * k + pp, 2 * z + cc))
    for s in (-1, 1):
        @pl.when(has_z[s])
        def _():
            for cc in range(2):
                greet(device(tm, 2 * (z + s) + cc))

        @pl.when(has_k[s])
        def _():
            greet(device(tm + 2 * s, sp))
    count = 3
    for s in (-1, 1):
        count = count + 2 * has_z[s].astype(jnp.int32) + has_k[s].astype(jnp.int32)
    pl.semaphore_wait(barrier, count)

    sent = []

    def send(cond, src, dst, sem, dev):
        copy = pltpu.make_async_remote_copy(
            src_ref=src, dst_ref=dst, send_sem=send_sem.at[len(sent)], recv_sem=sem,
            device_id=dev, device_id_type=MESH)
        if cond is None:
            copy.start()
        else:
            pl.when(cond)(copy.start)
        sent.append((cond, copy))

    def to_quad(own, src, dst, sem, pp, cc):
        if own:
            pltpu.make_async_copy(src, dst, sem).start()
        else:
            send(None, src, dst, sem, device(2 * k + pp, 2 * z + cc))

    def arrived(ref, sem):
        pltpu.make_async_copy(ref, ref, sem).wait()

    mine = pl.ds(2 + 2 * p, 2)
    other = pl.ds(4 - 2 * p, 2)
    inputs = (k_ref, v_ref)

    def deal_kv(j):
        for own, pp, cc in quad():
            for i in range(2):
                to_quad(own, inputs[i].at[:, :, cols(pp, cc, j)], kv.at[j, i, mine, 2 + c],
                        near.at[j], pp, cc)

    def deal_q(j):
        for own, pp, cc in quad():
            to_quad(own, q_ref.at[:, :, cols(pp, cc, j)], qb.at[j, pl.ds(2 * p, 2), c],
                    qsem.at[j], pp, cc)

    def along_z(j, i):
        for s in (-1, 1):
            tile = c if s == 1 else 4 + c
            for cc in range(2):
                send(has_z[s], inputs[i].at[:, :, cols(p, cc, j)], kv.at[j, i, mine, tile],
                     zsem.at[j, (1 - s) // 2], device(tm, 2 * (z + s) + cc))

    last = nh - 1
    deal_kv(0)
    along_z(0, 0)
    along_z(0, 1)
    deal_q(0)
    for j in range(1, nh):
        deal_kv(j)
        deal_q(j)
        if j == 1:
            along_z(1, 0)

    for f in range(2):
        row = 0
        for d, e, n in SEGMENTS:
            for t in range(n):
                kept = m_ref[f, 0, TR + d, W + e + t] > 0
                bias[f, row:row + 1, :] = jnp.full((1, BLK), jnp.where(kept, 0.0, -jnp.inf))
                row += 1
        bias[f, row:, :] = jnp.zeros((ROWS - row, BLK), jnp.float32)
    for own, pp, cc in quad():
        to_quad(own, bias, bb.at[pl.ds(2 * p, 2), c], bsem, pp, cc)

    for s in (-1, 1):
        tiles = slice(0, 2) if s == -1 else slice(4, 6)
        tile = 1 if s == -1 else 4
        frames = slice(0, 2) if s == -1 else slice(6, 8)
        frame = 1 if s == -1 else 6

        @pl.when(jnp.logical_not(has_z[s]))
        def _():
            for j in range(nh):
                for i in range(2):
                    kv[j, i, 2:6, tiles] = jnp.zeros((4, 2, BLK, HD), kv.dtype)
                    for f in (1, 6):
                        kv[j, i, f, tile] = jnp.zeros((BLK, HD), kv.dtype)

        @pl.when(jnp.logical_not(has_k[s]))
        def _():
            for j in range(nh):
                for i in range(2):
                    kv[j, i, frames, 2:4] = jnp.zeros((2, 2, BLK, HD), kv.dtype)

        for u in (-1, 1):
            @pl.when(jnp.logical_and(jnp.logical_not(has_k[s]), has_z[u]))
            def _():
                for j in range(nh):
                    for i in range(2):
                        kv[j, i, frame, 1 if u == -1 else 4] = jnp.zeros((BLK, HD), kv.dtype)

    def forward(j):
        arrived(kv.at[j, :, 2:6, 2:4], near.at[j])
        pieces = ((other, zsem.at[j]),)
        if j == last:
            pieces = ((pl.ds(4 - p, 1), zsem.at[j]), (pl.ds(5 - 3 * p, 1), dsem))
        for frames, sem in pieces:
            for s in (-1, 1):
                tiles = pl.ds(0 if s == 1 else 4, 2)
                send(has_z[s], kv.at[j, :, frames, pl.ds(2, 2)], kv.at[j, :, frames, tiles],
                     sem.at[(1 - s) // 2], device(tm, 2 * (z + s) + c))
        for s in (-1, 1):
            source, target = (4, 0) if s == 1 else (2, 6)
            send(has_k[s], kv.at[j, :, pl.ds(source, 2), pl.ds(2, 2)],
                 kv.at[j, :, pl.ds(target, 2), pl.ds(2, 2)],
                 ysem.at[j, (1 - s) // 2], device(tm + 2 * s, sp))

    factor = math.log2(math.e) / math.sqrt(HD)

    def attend(j, f, b):
        query = qb[j, f, b]
        parts, row = [], 0
        best = None
        for d, e, n in SEGMENTS:
            keys = kv[j, 0, f + 2 + d, b + 2 + e:b + 2 + e + n].reshape(n * BLK, HD)
            scores = lax.dot_general(query, keys, (((1,), (1,)), ((), ())),
                                     preferred_element_type=jnp.float32)
            for t in range(n):
                part = scores[:, t * BLK:(t + 1) * BLK] + bb[f, b, row:row + 1, :]
                parts.append(part)
                best = part if best is None else jnp.maximum(best, part)
                row += 1
        row_max = jnp.max(best, axis=1, keepdims=True)
        total, summed, at = None, None, 0
        for d, e, n in SEGMENTS:
            rounded = []
            for t in range(n):
                weights = jnp.exp2((parts[at] - row_max) * factor)
                total = weights if total is None else total + weights
                rounded.append(weights.astype(jnp.bfloat16))
                at += 1
            rounded = rounded[0] if n == 1 else jnp.concatenate(rounded, axis=1)
            vals = kv[j, 1, f + 2 + d, b + 2 + e:b + 2 + e + n].reshape(n * BLK, HD)
            product = jnp.dot(rounded, vals, preferred_element_type=jnp.float32)
            summed = product if summed is None else summed + product
        denominator = jnp.sum(total, axis=1, keepdims=True)
        ob[j, f, b] = (summed / denominator).astype(jnp.bfloat16)

    k_to = {0: jnp.where(p == 0, has_k[-1], has_k[1]), 1: jnp.where(p == 0, has_k[1], has_k[-1])}

    def corners(j, far):
        u = 1 - 2 * p if far else 2 * p - 1
        source, target = (5 - 3 * p, 1 + 5 * p) if far else (2 + 3 * p, 6 - 5 * p)
        for side, tile in ((0, 1), (1, 4)):
            send(jnp.logical_and(has_z[2 * side - 1], k_to[far]), kv.at[j, :, source, tile],
                 kv.at[j, :, target, tile], fsem.at[j, far, side], device(tm + 2 * u, sp))

    def corners_arrived(j, far):
        target = 1 + 5 * p if far else 6 - 5 * p
        for side, tile in ((0, 1), (1, 4)):
            @pl.when(jnp.logical_and(has_z[2 * side - 1], k_to[1 - far]))
            def _():
                arrived(kv.at[j, :, target, tile], fsem.at[j, far, side])

    def z_arrived(j, frames, sems):
        for side in range(2):
            @pl.when(has_z[2 * side - 1])
            def _():
                arrived(kv.at[j, :, frames, pl.ds(4 * side, 2)], sems.at[side])

    def rest_arrived(j):
        if j == 0:
            arrived(bb, bsem)
        arrived(qb.at[j], qsem.at[j])
        for u in (-1, 1):
            @pl.when(has_k[u])
            def _():
                arrived(kv.at[j, :, pl.ds(0 if u == -1 else 6, 2), pl.ds(2, 2)],
                        ysem.at[j, (1 + u) // 2])

    def head(j):
        z_arrived(j, pl.ds(2, 4), zsem.at[j])
        corners(j, 0)
        corners(j, 1)
        rest_arrived(j)
        corners_arrived(j, 0)
        corners_arrived(j, 1)

        def frame_step(f, carry):
            for b in range(2):
                attend(j, f, b)
            return carry

        lax.fori_loop(0, 4, frame_step, 0)
        for own, pp, cc in quad():
            to_quad(own, ob.at[j, pl.ds(2 * pp, 2), cc], o_ref.at[:, :, cols(p, c, j)],
                    osem, pp, cc)

    def last_frame(g):
        f = g + p * (3 - 2 * g)
        for b in range(2):
            attend(last, f, b)
        far = g // 2
        pp = p + far * (1 - 2 * p)
        for cc_own in (1, 0):
            cc = c if cc_own else 1 - c
            to_quad(cc_own and not far, ob.at[last, f, cc], o_ref.at[f - 2 * pp, :, cols(p, c, last)],
                    osem, pp, cc)

    forward(0)
    along_z(1, 1)
    for j in range(2, nh):
        along_z(j, 0)
    forward(1)
    for j in range(2, nh):
        along_z(j, 1)
    for j in range(nh - 1):
        head(j)
        if j + 2 < nh:
            forward(j + 2)
    z_arrived(last, pl.ds(2 + p, 3), zsem.at[last])
    corners(last, 0)
    rest_arrived(last)
    last_frame(1)
    z_arrived(last, pl.ds(5 - 3 * p, 1), dsem)
    corners(last, 1)
    last_frame(2)
    corners_arrived(last, 0)
    last_frame(3)
    corners_arrived(last, 1)
    last_frame(0)

    arrived(o_ref, osem)
    for cond, copy in sent:
        if cond is None:
            copy.wait_send()
        else:
            pl.when(cond)(copy.wait_send)


def on_device(groups, chips, queries, keys, values, tile_mask):
    nh = queries.shape[2] // HD // 4
    hbm = pl.BlockSpec(memory_space=pltpu.HBM)
    smem = pl.BlockSpec(memory_space=pltpu.SMEM)
    dma = pltpu.SemaphoreType.DMA
    return pl.pallas_call(
        functools.partial(kernel, groups, chips, nh),
        out_shape=jax.ShapeDtypeStruct(queries.shape, queries.dtype),
        in_specs=[hbm, hbm, hbm, smem],
        out_specs=pl.BlockSpec(memory_space=pl.ANY),
        scratch_shapes=[
            pltpu.VMEM((nh, 2, 8, 6, BLK, HD), jnp.bfloat16),
            pltpu.VMEM((nh, 4, 2, BLK, HD), jnp.bfloat16),
            pltpu.VMEM((4, 2, ROWS, BLK), jnp.float32),
            pltpu.VMEM((2, ROWS, BLK), jnp.float32),
            pltpu.VMEM((nh, 4, 2, BLK, HD), jnp.bfloat16),
            dma((32 * nh + 16,)),
            dma((nh,)),
            dma((nh, 2)),
            dma((2,)),
            dma((nh, 2)),
            dma((nh, 2, 2)),
            dma((nh,)),
            dma,
            dma,
        ],
        compiler_params=pltpu.CompilerParams(
            collective_id=0, has_side_effects=True, vmem_limit_bytes=60 * 2**20
        ),
    )(queries, keys, values, tile_mask)


def solution(mesh):
    in_specs = (
        P("tm", "space", None),
        P("tm", "space", None),
        P("tm", "space", None),
        P("tm", "space", None, None),
    )
    out_specs = P("tm", "space", None)
    return jax.shard_map(
        functools.partial(on_device, mesh.shape["tm"] // 2, mesh.shape["space"] // 2),
        mesh=mesh, in_specs=in_specs, out_specs=out_specs, check_vma=False
    )
```

```python
import functools
import math

import jax
import jax.numpy as jnp
from jax import lax
from jax.experimental import pallas as pl
from jax.experimental.pallas import tpu as pltpu
from jax.sharding import PartitionSpec as P

HD = 128
BLK = 128
TR = 2
W = 2
MESH = pl.DeviceIdType.MESH
SEGMENTS = ((0, -2, 5), (-1, -1, 3), (1, -1, 3), (-2, 0, 1), (2, 0, 1))
ROWS = 16


def kernel(groups, chips, nh, q_ref, k_ref, v_ref, m_ref, o_ref,
           kv, qb, bb, bias, ob, send_sem, near, zsem, dsem, ysem, fsem, qsem, bsem, osem):
    tm, sp = lax.axis_index("tm"), lax.axis_index("space")
    k, p = tm // 2, tm % 2
    z, c = sp // 2, sp % 2
    has_z = {-1: z > 0, 1: z < chips - 1}
    has_k = {-1: k > 0, 1: k < groups - 1}

    def device(t, s):
        return {"tm": t, "space": s}

    def cols(pp, cc, j):
        return pl.ds(pl.multiple_of(((2 * pp + cc) * nh + j) * HD, HD), HD)

    def quad():
        for dp, dc in ((0, 0), (0, 1), (1, 0), (1, 1)):
            yield dp + dc == 0, (p + dp) % 2, (c + dc) % 2

    barrier = pltpu.get_barrier_semaphore()

    def greet(dev):
        pl.semaphore_signal(barrier, inc=1, device_id=dev, device_id_type=MESH)

    for own, pp, cc in quad():
        if not own:
            greet(device(2 * k + pp, 2 * z + cc))
    for s in (-1, 1):
        @pl.when(has_z[s])
        def _():
            for cc in range(2):
                greet(device(tm, 2 * (z + s) + cc))

        @pl.when(has_k[s])
        def _():
            greet(device(tm + 2 * s, sp))
    count = 3
    for s in (-1, 1):
        count = count + 2 * has_z[s].astype(jnp.int32) + has_k[s].astype(jnp.int32)
    pl.semaphore_wait(barrier, count)

    sent = []

    def send(cond, src, dst, sem, dev):
        copy = pltpu.make_async_remote_copy(
            src_ref=src, dst_ref=dst, send_sem=send_sem.at[len(sent)], recv_sem=sem,
            device_id=dev, device_id_type=MESH)
        if cond is None:
            copy.start()
        else:
            pl.when(cond)(copy.start)
        sent.append((cond, copy))

    def to_quad(own, src, dst, sem, pp, cc):
        if own:
            pltpu.make_async_copy(src, dst, sem).start()
        else:
            send(None, src, dst, sem, device(2 * k + pp, 2 * z + cc))

    def arrived(ref, sem):
        pltpu.make_async_copy(ref, ref, sem).wait()

    mine = pl.ds(2 + 2 * p, 2)
    other = pl.ds(4 - 2 * p, 2)
    inputs = (k_ref, v_ref)

    def deal_kv(j):
        for own, pp, cc in quad():
            for i in range(2):
                to_quad(own, inputs[i].at[:, :, cols(pp, cc, j)], kv.at[j, i, mine, 2 + c],
                        near.at[j], pp, cc)

    def deal_q(j):
        for own, pp, cc in quad():
            to_quad(own, q_ref.at[:, :, cols(pp, cc, j)], qb.at[j, pl.ds(2 * p, 2), c],
                    qsem.at[j], pp, cc)

    def along_z(j, i):
        for s in (-1, 1):
            tile = c if s == 1 else 4 + c
            for cc in range(2):
                send(has_z[s], inputs[i].at[:, :, cols(p, cc, j)], kv.at[j, i, mine, tile],
                     zsem.at[j, (1 - s) // 2], device(tm, 2 * (z + s) + cc))

    last = nh - 1
    deal_kv(0)
    along_z(0, 0)
    along_z(0, 1)
    deal_q(0)
    for j in range(1, nh):
        deal_kv(j)
        if j == 1:
            along_z(1, 0)
    for j in range(1, nh):
        deal_q(j)

    for f in range(2):
        row = 0
        for d, e, n in SEGMENTS:
            for t in range(n):
                kept = m_ref[f, 0, TR + d, W + e + t] > 0
                bias[f, row:row + 1, :] = jnp.full((1, BLK), jnp.where(kept, 0.0, -jnp.inf))
                row += 1
        bias[f, row:, :] = jnp.zeros((ROWS - row, BLK), jnp.float32)
    for own, pp, cc in quad():
        to_quad(own, bias, bb.at[pl.ds(2 * p, 2), c], bsem, pp, cc)

    for s in (-1, 1):
        tiles = slice(0, 2) if s == -1 else slice(4, 6)
        tile = 1 if s == -1 else 4
        frames = slice(0, 2) if s == -1 else slice(6, 8)
        frame = 1 if s == -1 else 6

        @pl.when(jnp.logical_not(has_z[s]))
        def _():
            for j in range(nh):
                for i in range(2):
                    kv[j, i, 2:6, tiles] = jnp.zeros((4, 2, BLK, HD), kv.dtype)
                    for f in (1, 6):
                        kv[j, i, f, tile] = jnp.zeros((BLK, HD), kv.dtype)

        @pl.when(jnp.logical_not(has_k[s]))
        def _():
            for j in range(nh):
                for i in range(2):
                    kv[j, i, frames, 2:4] = jnp.zeros((2, 2, BLK, HD), kv.dtype)

        for u in (-1, 1):
            @pl.when(jnp.logical_and(jnp.logical_not(has_k[s]), has_z[u]))
            def _():
                for j in range(nh):
                    for i in range(2):
                        kv[j, i, frame, 1 if u == -1 else 4] = jnp.zeros((BLK, HD), kv.dtype)

    def forward(j):
        arrived(kv.at[j, :, 2:6, 2:4], near.at[j])
        pieces = ((other, zsem.at[j]),)
        if j == last:
            pieces = ((pl.ds(4 - p, 1), zsem.at[j]), (pl.ds(5 - 3 * p, 1), dsem))
        for frames, sem in pieces:
            for s in (-1, 1):
                tiles = pl.ds(0 if s == 1 else 4, 2)
                send(has_z[s], kv.at[j, :, frames, pl.ds(2, 2)], kv.at[j, :, frames, tiles],
                     sem.at[(1 - s) // 2], device(tm, 2 * (z + s) + c))
        for s in (-1, 1):
            source, target = (4, 0) if s == 1 else (2, 6)
            send(has_k[s], kv.at[j, :, pl.ds(source, 2), pl.ds(2, 2)],
                 kv.at[j, :, pl.ds(target, 2), pl.ds(2, 2)],
                 ysem.at[j, (1 - s) // 2], device(tm + 2 * s, sp))

    factor = math.log2(math.e) / math.sqrt(HD)

    def attend(j, f, b):
        query = qb[j, f, b]
        parts, row = [], 0
        best = None
        for d, e, n in SEGMENTS:
            keys = kv[j, 0, f + 2 + d, b + 2 + e:b + 2 + e + n].reshape(n * BLK, HD)
            scores = lax.dot_general(query, keys, (((1,), (1,)), ((), ())),
                                     preferred_element_type=jnp.float32)
            for t in range(n):
                part = scores[:, t * BLK:(t + 1) * BLK] + bb[f, b, row:row + 1, :]
                parts.append(part)
                best = part if best is None else jnp.maximum(best, part)
                row += 1
        row_max = jnp.max(best, axis=1, keepdims=True)
        total, summed, at = None, None, 0
        for d, e, n in SEGMENTS:
            rounded = []
            for t in range(n):
                weights = jnp.exp2((parts[at] - row_max) * factor)
                total = weights if total is None else total + weights
                rounded.append(weights.astype(jnp.bfloat16))
                at += 1
            rounded = rounded[0] if n == 1 else jnp.concatenate(rounded, axis=1)
            vals = kv[j, 1, f + 2 + d, b + 2 + e:b + 2 + e + n].reshape(n * BLK, HD)
            product = jnp.dot(rounded, vals, preferred_element_type=jnp.float32)
            summed = product if summed is None else summed + product
        denominator = jnp.sum(total, axis=1, keepdims=True)
        ob[j, f, b] = (summed / denominator).astype(jnp.bfloat16)

    k_to = {0: jnp.where(p == 0, has_k[-1], has_k[1]), 1: jnp.where(p == 0, has_k[1], has_k[-1])}

    def corners(j, far):
        u = 1 - 2 * p if far else 2 * p - 1
        source, target = (5 - 3 * p, 1 + 5 * p) if far else (2 + 3 * p, 6 - 5 * p)
        for side, tile in ((0, 1), (1, 4)):
            send(jnp.logical_and(has_z[2 * side - 1], k_to[far]), kv.at[j, :, source, tile],
                 kv.at[j, :, target, tile], fsem.at[j, far, side], device(tm + 2 * u, sp))

    def corners_arrived(j, far):
        target = 1 + 5 * p if far else 6 - 5 * p
        for side, tile in ((0, 1), (1, 4)):
            @pl.when(jnp.logical_and(has_z[2 * side - 1], k_to[1 - far]))
            def _():
                arrived(kv.at[j, :, target, tile], fsem.at[j, far, side])

    def z_arrived(j, frames, sems):
        for side in range(2):
            @pl.when(has_z[2 * side - 1])
            def _():
                arrived(kv.at[j, :, frames, pl.ds(4 * side, 2)], sems.at[side])

    def rest_arrived(j):
        if j == 0:
            arrived(bb, bsem)
        arrived(qb.at[j], qsem.at[j])
        for u in (-1, 1):
            @pl.when(has_k[u])
            def _():
                arrived(kv.at[j, :, pl.ds(0 if u == -1 else 6, 2), pl.ds(2, 2)],
                        ysem.at[j, (1 + u) // 2])

    def head(j):
        z_arrived(j, pl.ds(2, 4), zsem.at[j])
        corners(j, 0)
        corners(j, 1)
        if j + 2 < nh:
            forward(j + 2)
        rest_arrived(j)
        corners_arrived(j, 0)
        corners_arrived(j, 1)

        def frame_step(f, carry):
            for b in range(2):
                attend(j, f, b)
            return carry

        lax.fori_loop(0, 4, frame_step, 0)
        for own, pp, cc in quad():
            to_quad(own, ob.at[j, pl.ds(2 * pp, 2), cc], o_ref.at[:, :, cols(p, c, j)],
                    osem, pp, cc)

    def last_frame(g):
        f = g + p * (3 - 2 * g)
        for b in range(2):
            attend(last, f, b)
        far = g // 2
        pp = p + far * (1 - 2 * p)
        for cc_own in (1, 0):
            cc = c if cc_own else 1 - c
            to_quad(cc_own and not far, ob.at[last, f, cc], o_ref.at[f - 2 * pp, :, cols(p, c, last)],
                    osem, pp, cc)

    forward(0)
    along_z(1, 1)
    for j in range(2, nh):
        along_z(j, 0)
    forward(1)
    for j in range(2, nh):
        along_z(j, 1)
    for j in range(nh - 1):
        head(j)
    z_arrived(last, pl.ds(2 + p, 3), zsem.at[last])
    corners(last, 0)
    rest_arrived(last)
    last_frame(1)
    z_arrived(last, pl.ds(5 - 3 * p, 1), dsem)
    corners(last, 1)
    last_frame(2)
    corners_arrived(last, 0)
    last_frame(3)
    corners_arrived(last, 1)
    last_frame(0)

    arrived(o_ref, osem)
    for cond, copy in sent:
        if cond is None:
            copy.wait_send()
        else:
            pl.when(cond)(copy.wait_send)


def on_device(groups, chips, queries, keys, values, tile_mask):
    nh = queries.shape[2] // HD // 4
    hbm = pl.BlockSpec(memory_space=pltpu.HBM)
    smem = pl.BlockSpec(memory_space=pltpu.SMEM)
    dma = pltpu.SemaphoreType.DMA
    return pl.pallas_call(
        functools.partial(kernel, groups, chips, nh),
        out_shape=jax.ShapeDtypeStruct(queries.shape, queries.dtype),
        in_specs=[hbm, hbm, hbm, smem],
        out_specs=pl.BlockSpec(memory_space=pl.ANY),
        scratch_shapes=[
            pltpu.VMEM((nh, 2, 8, 6, BLK, HD), jnp.bfloat16),
            pltpu.VMEM((nh, 4, 2, BLK, HD), jnp.bfloat16),
            pltpu.VMEM((4, 2, ROWS, BLK), jnp.float32),
            pltpu.VMEM((2, ROWS, BLK), jnp.float32),
            pltpu.VMEM((nh, 4, 2, BLK, HD), jnp.bfloat16),
            dma((32 * nh + 16,)),
            dma((nh,)),
            dma((nh, 2)),
            dma((2,)),
            dma((nh, 2)),
            dma((nh, 2, 2)),
            dma((nh,)),
            dma,
            dma,
        ],
        compiler_params=pltpu.CompilerParams(
            collective_id=0, has_side_effects=True, vmem_limit_bytes=60 * 2**20
        ),
    )(queries, keys, values, tile_mask)


def solution(mesh):
    in_specs = (
        P("tm", "space", None),
        P("tm", "space", None),
        P("tm", "space", None),
        P("tm", "space", None, None),
    )
    out_specs = P("tm", "space", None)
    return jax.shard_map(
        functools.partial(on_device, mesh.shape["tm"] // 2, mesh.shape["space"] // 2),
        mesh=mesh, in_specs=in_specs, out_specs=out_specs, check_vma=False
    )
```
